32 devices in a mesh: grp: 8 (over y, x, core), mlp: 4 (over z).
Axes of the slice: x: 2, y: 2, z: 4, core: 2. Of those that a mesh axis runs over, the one named last changes fastest.
Arguments:
- queries: bfloat16 [8, 128, 4096], P('grp'), may hold values from -70 to 70
- fresh_kv: bfloat16 [8, 128, 1024], P('grp', 'mlp'), may hold values from -5 to 5
- kv_pages: bfloat16 [8, 32, 128, 1024], P('grp', 'mlp'), may hold values from -5 to 5
- residual: bfloat16 [8, 128, 4096], P('grp'), may hold values from -3 to 3
- norm_gain: float32 [4096], replicated, may hold values from 0.5 to 1.5
- out_weight: bfloat16 [4096, 4096], P('mlp', 'grp'), may hold values from -0.09375 to 0.09375
- gate_weight: bfloat16 [4096, 6144], P('grp', 'mlp'), may hold values from -0.09375 to 0.09375
- up_weight: bfloat16 [4096, 6144], P('grp', 'mlp'), may hold values from -0.09375 to 0.09375
- down_weight: bfloat16 [6144, 4096], P('mlp', 'grp'), may hold values from -0.078125 to 0.078125
- page_table: int32 [8, 16, 12], P('grp'), may hold values from -1 to 31, as said below
- shared_pages: int32 [8, 4], P('grp'), may hold values from 0 to 31, as said below
- cache_lens: int32 [8, 16], P('grp'), may hold values from 513 to 2048, as said below
- prefill_offsets: int32 [8], P('grp'), may hold values from 1 to 512
Outputs:
- layer_out: bfloat16 [8, 128, 4096], P('grp', 'mlp')
The draws below stay inside these ranges and needn't reach their ends.
Inputs may be any that keep to these rules, and one draw needn't show every extreme that they name: `page_table`: row d lists the pool pages that hold decode d's tokens after the shared prompt, in order, and -1 after its last page; no page appears twice in a group, and none is also a shared page. `shared_pages`: the pool pages of the group's shared prompt in order; they are the first 4 pages of every request of the group. `cache_lens`: decode d's cached tokens fill exactly its listed pages after the 4 shared pages; in every group one decode has the most.
All inputs are finite; a program needn't handle non-finite values.
Results may differ from the reference program's by a relative error of at most 0.029.
Values may be sent and summed in bfloat16 or wider, within the bound.
A program may use at most 128 MiB of HBM per device.

```python
import jax
import jax.numpy as jnp
from jax import lax

D = 4096
HEADS = 32
KV_HEADS = 4
HEAD = 128
FF = 6144
PAGE = 128
PAGES = 32
SHARED_PAGES = 4
PRIVATE_PAGES = 12
DECODES = 16
PREFILL = 112
ROWS = 128
GROUPS = 8
N_MLP = 4


def page_plan(key):
    folded = jax.random.fold_in(key, 7)

    def one_group(group_key):
        key_order, key_longest, key_counts, key_tail = jax.random.split(group_key, 4)
        page_order = jax.random.permutation(key_order, PAGES).astype(jnp.int32)
        longest = jax.random.randint(key_longest, (), 0, DECODES).astype(jnp.int32)
        spread = (PAGES - SHARED_PAGES - PRIVATE_PAGES) // (DECODES - 1)
        decode_ids = jnp.arange(DECODES, dtype=jnp.int32)
        counts = jax.random.randint(key_counts, (DECODES,), 1, spread + 1).astype(jnp.int32)
        counts = jnp.where(decode_ids == longest, PRIVATE_PAGES, counts).astype(jnp.int32)
        starts = SHARED_PAGES + jnp.cumsum(counts, dtype=jnp.int32) - counts
        column = jnp.arange(PRIVATE_PAGES, dtype=jnp.int32)
        position = jnp.minimum(starts[:, None] + column[None, :], PAGES - 1)
        page_rows = jnp.where(column[None, :] < counts[:, None], jnp.take(page_order, position), -1)
        tail_len = jax.random.randint(key_tail, (DECODES,), 1, PAGE + 1).astype(jnp.int32)
        lengths = (SHARED_PAGES + counts - 1) * PAGE + tail_len
        lengths = jnp.where(decode_ids == longest, (SHARED_PAGES + PRIVATE_PAGES) * PAGE, lengths)
        return (page_rows.astype(jnp.int32), page_order[:SHARED_PAGES], lengths.astype(jnp.int32))
    return jax.vmap(one_group)(jax.random.split(folded, GROUPS))


def token_plan(key):
    folded = jax.random.fold_in(key, 11)
    key_query, key_fresh = jax.random.split(folded)
    query_shape = (GROUPS, ROWS, HEADS * HEAD)
    fresh_shape = (GROUPS, ROWS, 2 * KV_HEADS * HEAD)
    query_draw = jnp.clip(3.0 * jax.random.normal(key_query, query_shape, jnp.float32), -15.0, 15.0)
    fresh_draw = jnp.clip(jax.random.normal(key_fresh, fresh_shape, jnp.float32), -5.0, 5.0)
    return (query_draw, fresh_draw)


def draw_queries(key, part):
    return token_plan(key)[0].astype(jnp.bfloat16)


def draw_fresh_kv(key, part):
    return token_plan(key)[1].astype(jnp.bfloat16)


def draw_page_table(key, part):
    return page_plan(key)[0]


def draw_shared_pages(key, part):
    return page_plan(key)[1]


def draw_cache_lens(key, part):
    return page_plan(key)[2]


def place_ends(result, rng, least, high):
    extent = result.shape
    place = [jax.random.randint(jax.random.fold_in(rng, axis), (), 0, extent[axis]) for axis in range(len(extent))]
    result = result.at[tuple(place)].set(least)
    longest = extent.index(max(extent))
    place[longest] = (place[longest] + 1) % extent[longest]
    return result.at[tuple(place)].set(high)


def shard_levels(own_key, shape, cuts, low, largest):
    def one(dim, shards_of):
        steps = jax.random.uniform(jax.random.fold_in(jax.random.fold_in(own_key, 6), dim), (shards_of,), jnp.float32, low / len(cuts), largest / len(cuts))
        return jnp.repeat(jnp.exp(steps), shape[dim] // shards_of).reshape((-1,) + (1,) * (len(shape) - dim - 1))

    loudness = one(*cuts[0])
    for cut in cuts[1:]:
        loudness = loudness * one(*cut)
    return loudness


def gaussian(stream_key, extent, deviation, most, shards=(), kind=jnp.bfloat16):
    drawn = jax.random.normal(stream_key, extent, jnp.float32) * deviation
    if len(shards) > 0:
        drawn = shard_levels(stream_key, extent, shards, -0.22, 0.18) * drawn
    return jnp.clip(drawn, min=-most, max=most).astype(kind)


def setup_inputs(seed: int = 0) -> dict:
    key_of = jax.random.split(jax.random.key(seed), 14)
    return {
        "queries": draw_queries(jax.random.fold_in(key_of[13], 71), 0),
        "fresh_kv": draw_fresh_kv(jax.random.fold_in(key_of[13], 71), 0),
        "kv_pages": gaussian(key_of[2], (GROUPS, PAGES, PAGE, 2 * KV_HEADS * HEAD), 1.0, 5.0, ((0, 8), (1, 4))),
        "residual": gaussian(key_of[3], (GROUPS, ROWS, D), 0.5, 3.0, ((0, 8),)),
        "norm_gain": jnp.clip(jax.random.uniform(key_of[4], (D,), jnp.float32, 0.5, 1.5), 0.5, 1.5),
        "out_weight": gaussian(key_of[5], (HEADS * HEAD, D), (HEADS * HEAD) ** -0.5, 0.09375, ((0, 4), (1, 8))),
        "gate_weight": gaussian(key_of[6], (D, FF), D ** -0.5, 0.09375, ((0, 8), (1, 4))),
        "up_weight": gaussian(key_of[7], (D, FF), D ** -0.5, 0.09375, ((0, 8), (1, 4))),
        "down_weight": gaussian(key_of[8], (FF, D), FF ** -0.5, 0.078125, ((0, 4), (1, 8))),
        "page_table": draw_page_table(jax.random.fold_in(key_of[13], 71), 0),
        "shared_pages": draw_shared_pages(jax.random.fold_in(key_of[13], 71), 0),
        "cache_lens": draw_cache_lens(jax.random.fold_in(key_of[13], 71), 0),
        "prefill_offsets": place_ends(jax.random.randint(key_of[12], (GROUPS,), 1, SHARED_PAGES * PAGE + 1), jax.random.fold_in(key_of[12], 1), 1, SHARED_PAGES * PAGE).astype(jnp.int32),
    }


NEG_FILL = -1e+30
EPSILON = 1e-05

def page_layout(page_ids, table_group, shared_group):
    shared_match = shared_group[None, :] == page_ids[:, None]
    is_shared = jnp.any(shared_match, axis=1)
    shared_slot = lax.optimization_barrier(jnp.sum(jnp.where(shared_match, jnp.arange(SHARED_PAGES, dtype=jnp.int32)[None, :], 0), axis=1, dtype=jnp.int32))
    own_match = table_group[None, :, :] == page_ids[:, None, None]
    owner_id = lax.optimization_barrier(jnp.sum(jnp.where(own_match, jnp.arange(DECODES, dtype=jnp.int32)[None, :, None] + 1, 0), axis=(1, 2), dtype=jnp.int32)) - 1
    own_slot = lax.optimization_barrier(jnp.sum(jnp.where(own_match, jnp.arange(PRIVATE_PAGES, dtype=jnp.int32)[None, None, :], 0), axis=(1, 2), dtype=jnp.int32))
    page_base = jnp.where(is_shared, shared_slot * PAGE, (SHARED_PAGES + own_slot) * PAGE)
    key_pos = (page_base[:, None] + jnp.arange(PAGE, dtype=jnp.int32)[None, :]).reshape(-1)
    key_shared = jnp.repeat(is_shared, PAGE)
    key_owner = jnp.repeat(jnp.where(is_shared, -1, owner_id), PAGE)
    return (key_pos, key_shared, key_owner)

def row_layout(lens_group, offset_value):
    row_ids = jnp.arange(ROWS, dtype=jnp.int32)
    is_prefill = row_ids < PREFILL
    decode_id = jnp.where(is_prefill, -2, row_ids - PREFILL)
    picked = decode_id[:, None] == jnp.arange(DECODES, dtype=jnp.int32)[None, :]
    decode_limit = lax.optimization_barrier(jnp.sum(jnp.where(picked, lens_group[None, :], 0), axis=1, dtype=jnp.int32))
    limit = jnp.where(is_prefill, offset_value, decode_limit)
    return (row_ids, is_prefill, decode_id, limit)

def cache_visible(key_pos, key_shared, key_owner, decode_id, limit):
    belongs = key_shared[None, :] | (key_owner[None, :] == decode_id[:, None])
    return belongs & (key_pos[None, :] < limit[:, None])

def fresh_visible(key_rows, row_ids, is_prefill):
    before = (key_rows[None, :] < PREFILL) & (key_rows[None, :] <= row_ids[:, None])
    return jnp.where(is_prefill[:, None], before, key_rows[None, :] == row_ids[:, None])

def group_layer(inputs, out_full, gate_full, up_full, down_full, norm_gain):
    queries, fresh_kv, kv_pages, residual, page_table, shared_pages, cache_lens, prefill_offset = inputs
    key_pos, key_shared, key_owner = page_layout(jnp.arange(PAGES, dtype=jnp.int32), page_table, shared_pages)
    row_ids, is_prefill, decode_id, limit = row_layout(cache_lens, prefill_offset)
    visible = jnp.concatenate([cache_visible(key_pos, key_shared, key_owner, decode_id, limit), fresh_visible(row_ids, row_ids, is_prefill)], axis=1)
    cached = kv_pages.reshape(PAGES * PAGE, 2, KV_HEADS, HEAD)
    fresh = fresh_kv.reshape(ROWS, 2, KV_HEADS, HEAD)
    every_key = jnp.concatenate([cached, fresh], axis=0).astype(jnp.float32)
    grouped = HEADS // KV_HEADS
    query_heads = queries.astype(jnp.float32).reshape(ROWS, KV_HEADS, grouped, HEAD)
    score_scale = HEAD ** (-0.5)
    results = []
    for head_index in range(KV_HEADS):
        scores = jnp.einsum('rgh,kh->rgk', query_heads[:, head_index], every_key[:, 0, head_index]) * score_scale
        scores = jnp.where(visible[:, None, :], scores, NEG_FILL)
        row_peak = lax.optimization_barrier(jnp.max(scores, axis=2, keepdims=True))
        exponent = jnp.where(visible[:, None, :], jnp.exp(scores - row_peak), 0.0)
        row_total = lax.optimization_barrier(jnp.sum(exponent, axis=2, keepdims=True))
        rounded = lax.optimization_barrier(exponent.astype(jnp.bfloat16)).astype(jnp.float32)
        weighted = jnp.einsum('rgk,kh->rgh', rounded, every_key[:, 1, head_index])
        results.append(weighted / row_total)
    attended = jnp.stack(results, axis=1).reshape(ROWS, HEADS * HEAD).astype(jnp.bfloat16)
    feature_blocks = attended.astype(jnp.float32).reshape(ROWS, N_MLP, HEADS * HEAD // N_MLP)
    weight_blocks = out_full.reshape(N_MLP, HEADS * HEAD // N_MLP, D)
    partial_value = lax.optimization_barrier(jnp.einsum('rbf,bfd->brd', feature_blocks, weight_blocks).astype(jnp.bfloat16))
    projected = lax.optimization_barrier(jnp.sum(partial_value.astype(jnp.float32), axis=0))
    updated = residual.astype(jnp.float32) + projected
    normed = (updated * lax.rsqrt(lax.optimization_barrier(jnp.mean(updated * updated, axis=1, keepdims=True)) + EPSILON) * norm_gain).astype(jnp.bfloat16)
    normed_wide = normed.astype(jnp.float32)
    gate_act = jnp.dot(normed_wide, gate_full, preferred_element_type=jnp.float32)
    up_act = jnp.dot(normed_wide, up_full, preferred_element_type=jnp.float32)
    hidden = (jax.nn.silu(gate_act) * up_act).astype(jnp.bfloat16)
    hidden_blocks = hidden.astype(jnp.float32).reshape(ROWS, N_MLP, FF // N_MLP)
    down_blocks = down_full.reshape(N_MLP, FF // N_MLP, D)
    returned_parts = lax.optimization_barrier(jnp.einsum('rbf,bfd->brd', hidden_blocks, down_blocks).astype(jnp.bfloat16))
    returned = lax.optimization_barrier(jnp.sum(returned_parts.astype(jnp.float32), axis=0))
    return (updated + returned).astype(jnp.bfloat16)

def reference(queries, fresh_kv, kv_pages, residual, norm_gain, out_weight, gate_weight, up_weight, down_weight, page_table, shared_pages, cache_lens, prefill_offsets):
    out_full = out_weight.astype(jnp.float32)
    gate_full = gate_weight.astype(jnp.float32)
    up_full = up_weight.astype(jnp.float32)
    down_full = down_weight.astype(jnp.float32)

    def one_group(inputs):
        return group_layer(inputs, out_full, gate_full, up_full, down_full, norm_gain)
    return lax.map(one_group, (queries, fresh_kv, kv_pages, residual, page_table, shared_pages, cache_lens, prefill_offsets))
```

```python
import functools

import jax
import jax.numpy as jnp
from jax import lax
from jax.experimental import pallas as pl
from jax.experimental.pallas import tpu as pltpu
from jax.sharding import PartitionSpec as P

HEADS = 32
KV_HEADS = 4
HEAD = 128
PAGE = 128
SHARED_PAGES = 4
PRIVATE_PAGES = 12
DECODES = 16
PREFILL = 112
ROWS = 128
GROUPED = HEADS // KV_HEADS

NEG_FILL = -1e30
EPSILON = 1e-05
MESH = pl.DeviceIdType.MESH
F32 = jnp.float32
BF16 = jnp.bfloat16


def tile_of(width):
    return 256 if width % 256 == 0 else 128


def kernel(
    n,
    chips,
    queries,
    kv_pages,
    fresh_kv,
    gain,
    table,
    shared,
    lens,
    offset,
    residual,
    out_weight,
    gate_weight,
    up_weight,
    down_weight,
    out,
    bias,
    fresh_bias,
    part_send,
    part_recv,
    stat_send,
    stat_recv,
    res,
    out_w,
    gate_w,
    up_w,
    down_w,
    att,
    proj_part,
    proj_recv,
    proj,
    upd,
    normed,
    gu,
    gu_recv,
    ssq,
    ssq_recv,
    hid,
    down_part,
    down_recv,
    fin,
    fin_recv,
    weight_local,
    weight_send,
    weight_recv,
    res_local,
    res_send,
    res_recv,
    part_ss,
    part_rs,
    stat_ss,
    stat_rs,
    att_ss,
    att_rs,
    rs_ss,
    rs_rs,
    ag_ss,
    ag_rs,
    gu_ss,
    gu_rs,
    ssq_ss,
    ssq_rs,
    hid_ss,
    hid_rs,
    down_ss,
    down_rs,
    fin_ss,
    fin_rs,
):
    me = lax.axis_index("mlp")
    grp = lax.axis_index("grp")
    chip = grp // 2
    core = grp % 2
    parts = res.shape[0]
    piece = res.shape[3]
    width = out_w.shape[2]
    cols = 2 * width
    feats = att.shape[-1]
    hidden = hid.shape[-1]
    block_heads = feats // HEAD
    rows = n * chips * piece

    def along(j):
        return {"mlp": lax.rem(me + j, n)}

    def across(j):
        return {"grp": lax.rem(chip + j, chips) * 2 + core}

    def back(j):
        return {"grp": lax.rem(chip + chips - j, chips) * 2 + core}

    partner = {"grp": chip * 2 + (1 - core)}

    def send(src, dst, ss, rs, device):
        copy = pltpu.make_async_remote_copy(
            src_ref=src,
            dst_ref=dst,
            send_sem=ss,
            recv_sem=rs,
            device_id=device,
            device_id_type=MESH,
        )
        copy.start()
        return copy

    barrier = pltpu.get_barrier_semaphore()
    for j in range(1, n):
        pl.semaphore_signal(barrier, inc=1, device_id=along(j), device_id_type=MESH)
    for j in range(1, chips):
        pl.semaphore_signal(barrier, inc=1, device_id=across(j), device_id_type=MESH)
    pl.semaphore_signal(barrier, inc=1, device_id=partner, device_id_type=MESH)

    local_weights = (
        (out_weight, out_w.at[core]),
        (gate_weight, gate_w.at[core]),
        (up_weight, up_w.at[core]),
        (down_weight, down_w.at[core]),
    )
    held = []
    for i, (src, dst) in enumerate(local_weights):
        copy = pltpu.make_async_copy(src, dst, weight_local.at[i])
        copy.start()
        held.append(copy)
    own_res = []
    for q in range(parts):
        copy = pltpu.make_async_copy(
            residual.at[:, q, :, pl.ds(pl.multiple_of(chip * cols, cols), cols)],
            res.at[q, :, 0],
            res_local.at[q],
        )
        copy.start()
        own_res.append(copy)

    pl.semaphore_wait(barrier, n + chips - 1)

    paired = []
    for i, (src, dst) in enumerate(local_weights):
        paired.append(send(src, dst, weight_send.at[i], weight_recv.at[i], partner))
    res_copies = []
    for q in range(parts):
        for j in range(1, chips):
            start = pl.multiple_of(lax.rem(chip + j, chips) * cols, cols)
            res_copies.append(
                send(
                    residual.at[:, q, :, pl.ds(start, cols)],
                    res.at[q, :, j],
                    res_send.at[q, j],
                    res_recv.at[q, j],
                    across(j),
                )
            )

    pool_pages = kv_pages.shape[0] // PAGE
    own_count = fresh_kv.shape[0]
    token = lax.broadcasted_iota(jnp.int32, (1, PAGE), 1)
    slot_ids = lax.broadcasted_iota(jnp.int32, (DECODES, PRIVATE_PAGES), 1)
    shared_ids = lax.broadcasted_iota(jnp.int32, (1, SHARED_PAGES), 1)
    for p in range(pool_pages):
        page_id = me * pool_pages + p
        own = table[...] == page_id
        own_any = jnp.max(jnp.where(own, 1, 0), axis=1, keepdims=True)
        own_base = jnp.sum(
            jnp.where(own, (SHARED_PAGES + slot_ids) * PAGE, 0), axis=1, keepdims=True
        )
        match = shared[...] == page_id
        is_shared = jnp.max(jnp.where(match, 1, 0), axis=1, keepdims=True)
        shared_base = jnp.sum(jnp.where(match, shared_ids * PAGE, 0), axis=1, keepdims=True)
        position = shared_base + token
        seen = (is_shared > 0) & (position < offset[...])
        bias[0:PREFILL, p * PAGE : (p + 1) * PAGE] = jnp.broadcast_to(
            jnp.where(seen, 0.0, NEG_FILL), (PREFILL, PAGE)
        )
        belongs = jnp.maximum(own_any, is_shared)
        base = jnp.where(is_shared > 0, shared_base, own_base)
        seen = (belongs > 0) & (base + token < lens[...])
        bias[PREFILL:ROWS, p * PAGE : (p + 1) * PAGE] = jnp.where(seen, 0.0, NEG_FILL)
    row_ids = lax.broadcasted_iota(jnp.int32, (ROWS, own_count), 0)
    key_rows = me * own_count + lax.broadcasted_iota(jnp.int32, (ROWS, own_count), 1)
    seen = ((row_ids < PREFILL) & (key_rows < PREFILL) & (key_rows <= row_ids)) | (
        (row_ids >= PREFILL) & (key_rows == row_ids)
    )
    fresh_bias[...] = jnp.where(seen, 0.0, NEG_FILL)

    lane = lax.broadcasted_iota(jnp.int32, (ROWS, HEAD), 1)
    scale = HEAD ** (-0.5)
    keys_across = (((1,), (1,)), ((), ()))
    value_at = KV_HEADS * HEAD

    part_copies = []
    stat_copies = []
    for j in range(1, n + 1):
        block = lax.rem(me + j, n)

        def one_head(i, stats, block=block):
            head = block * block_heads + i
            key_start = pl.multiple_of((head // GROUPED) * HEAD, HEAD)
            query = queries[:, pl.ds(pl.multiple_of(head * HEAD, HEAD), HEAD)]
            scores = (
                lax.dot_general(
                    query,
                    kv_pages[:, pl.ds(key_start, HEAD)],
                    keys_across,
                    preferred_element_type=F32,
                )
                * scale
                + bias[...]
            )
            fresh_scores = (
                lax.dot_general(
                    query,
                    fresh_kv[:, pl.ds(key_start, HEAD)],
                    keys_across,
                    preferred_element_type=F32,
                )
                * scale
                + fresh_bias[...]
            )
            peak = jnp.maximum(
                jnp.max(scores, axis=1, keepdims=True),
                jnp.max(fresh_scores, axis=1, keepdims=True),
            )
            exps = jnp.exp(scores - peak)
            fresh_exps = jnp.exp(fresh_scores - peak)
            total = jnp.sum(exps, axis=1, keepdims=True) + jnp.sum(
                fresh_exps, axis=1, keepdims=True
            )
            mixed = jnp.dot(
                exps.astype(BF16),
                kv_pages[:, pl.ds(value_at + key_start, HEAD)],
                preferred_element_type=F32,
            ) + jnp.dot(
                fresh_exps.astype(BF16),
                fresh_kv[:, pl.ds(value_at + key_start, HEAD)],
                preferred_element_type=F32,
            )
            part_send[block, :, pl.ds(pl.multiple_of(i * HEAD, HEAD), HEAD)] = (
                mixed / total
            ).astype(BF16)
            return jnp.where(lane == i, peak + jnp.log(total), stats)

        stats = lax.fori_loop(0, block_heads, one_head, jnp.zeros((ROWS, HEAD), F32), unroll=2)
        stat_send[block] = stats.T[0:8]
        if j < n:
            part_copies.append(
                send(part_send.at[block], part_recv.at[j], part_ss.at[j], part_rs.at[j], along(j))
            )
            stat_copies.append(
                send(stat_send.at[block], stat_recv.at[j], stat_ss.at[j], stat_rs.at[j], along(j))
            )

    for copy in stat_copies + part_copies:
        copy.wait_recv()
    levels = [stat_send[me].T] + [stat_recv[j].T for j in range(1, n)]
    top = functools.reduce(jnp.maximum, levels)
    shares = [jnp.exp(level - top) for level in levels]
    whole = functools.reduce(jnp.add, shares)
    shares = [share / whole for share in shares]
    for i in range(block_heads):
        span = slice(i * HEAD, (i + 1) * HEAD)
        value = part_send[me, :, span].astype(F32) * shares[0][:, i : i + 1]
        for j in range(1, n):
            value = value + part_recv[j, :, span].astype(F32) * shares[j][:, i : i + 1]
        value = value.astype(BF16).reshape(n, parts, piece, HEAD)
        for q in range(parts):
            att[q, :, 0, :, span] = value[:, q]
    att_copies = [[] for _ in range(parts)]
    for q in range(parts):
        for j in range(1, chips):
            att_copies[q].append(
                send(att.at[q, :, 0], att.at[q, :, j], att_ss.at[q, j], att_rs.at[q, j], across(j))
            )

    held[0].wait()
    paired[0].wait_recv()
    rs_copies = [[] for _ in range(parts)]
    tile = tile_of(width)
    for q in range(parts):
        for copy in att_copies[q]:
            copy.wait_recv()
        for half in range(2):

            @pl.loop(0, width // tile)
            def _(t, q=q, half=half):
                at = pl.multiple_of(t * tile, tile)
                value = jnp.dot(
                    att[q].reshape(rows, feats),
                    out_w[half, :, pl.ds(at, tile)],
                    preferred_element_type=F32,
                )
                proj_part[q, :, :, :, pl.ds(pl.multiple_of(half * width + at, tile), tile)] = (
                    value.astype(BF16).reshape(n, chips, piece, tile)
                )

        for j in range(1, n):
            rs_copies[q].append(
                send(
                    proj_part.at[q, lax.rem(me + j, n)],
                    proj_recv.at[q, j],
                    rs_ss.at[q, j],
                    rs_rs.at[q, j],
                    along(j),
                )
            )
    ag_copies = [[] for _ in range(parts)]
    for q in range(parts):
        for copy in rs_copies[q]:
            copy.wait_recv()
        value = proj_part[q, me].astype(F32)
        for j in range(1, n):
            value = value + proj_recv[q, j].astype(F32)
        proj[q, me] = value.astype(BF16)
        for j in range(1, n):
            ag_copies[q].append(
                send(proj.at[q, me], proj.at[q, me], ag_ss.at[q, j], ag_rs.at[q, j], along(j))
            )

    for copy in own_res:
        copy.wait()
    for copy in res_copies:
        copy.wait_recv()
    for i in (1, 2):
        held[i].wait()
        paired[i].wait_recv()
    gain_here = gain[:, pl.ds(pl.multiple_of(chip * cols, cols), cols)]
    gu_copies = [[] for _ in range(parts)]
    tile = tile_of(hidden)
    for q in range(parts):
        for j in range(1, n):
            other = lax.rem(me + n - j, n)
            pltpu.make_async_remote_copy(
                src_ref=proj.at[q, other],
                dst_ref=proj.at[q, other],
                send_sem=ag_ss.at[q, j],
                recv_sem=ag_rs.at[q, j],
                device_id=along(j),
                device_id_type=MESH,
            ).wait_recv()

        @pl.loop(0, n)
        def _(p, q=q):
            value = res[q, p].astype(F32) + proj[q, p].astype(F32)
            upd[q, p] = value
            square = jnp.sum(value * value, axis=2, keepdims=True)
            ssq[q, p] = jnp.broadcast_to(square, (chips, piece, HEAD))
            normed[q, p] = (value * gain_here[None]).astype(BF16)

        for j in range(1, chips):
            gu_copies[q].append(
                send(ssq.at[q, :, j], ssq_recv.at[q, j], ssq_ss.at[q, j], ssq_rs.at[q, j], back(j))
            )
        for which, weight in enumerate((gate_w, up_w)):

            @pl.loop(0, hidden // tile)
            def _(t, q=q, which=which, weight=weight):
                at = pl.multiple_of(t * tile, tile)
                value = jnp.dot(
                    normed[q].reshape(rows, cols),
                    weight[:, :, pl.ds(at, tile)].reshape(cols, tile),
                    preferred_element_type=F32,
                )
                gu[q, which, :, :, :, pl.ds(at, tile)] = value.astype(BF16).reshape(
                    n, chips, piece, tile
                )

            for j in range(1, chips):
                gu_copies[q].append(
                    send(
                        gu.at[q, which, :, j],
                        gu_recv.at[q, j, which],
                        gu_ss.at[q, j, which],
                        gu_rs.at[q, j, which],
                        back(j),
                    )
                )

    hid_copies = [[] for _ in range(parts)]
    for q in range(parts):
        for copy in gu_copies[q]:
            copy.wait_recv()

        @pl.loop(0, n)
        def _(p, q=q):
            square = ssq[q, p, 0]
            for j in range(1, chips):
                square = square + ssq_recv[q, j, p]
            factor = lax.rsqrt(square[:, 0:1] / (chips * cols) + EPSILON)
            gate = gu[q, 0, p, 0].astype(F32)
            up = gu[q, 1, p, 0].astype(F32)
            for j in range(1, chips):
                gate = gate + gu_recv[q, j, 0, p].astype(F32)
                up = up + gu_recv[q, j, 1, p].astype(F32)
            gate = gate * factor
            up = up * factor
            hid[q, p, 0] = (gate / (1.0 + jnp.exp(-gate)) * up).astype(BF16)

        for j in range(1, chips):
            hid_copies[q].append(
                send(hid.at[q, :, 0], hid.at[q, :, j], hid_ss.at[q, j], hid_rs.at[q, j], across(j))
            )

    held[3].wait()
    paired[3].wait_recv()
    down_copies = [[] for _ in range(parts)]
    tile = tile_of(width)
    for q in range(parts):
        for copy in hid_copies[q]:
            copy.wait_recv()
        for half in range(2):

            @pl.loop(0, width // tile)
            def _(t, q=q, half=half):
                at = pl.multiple_of(t * tile, tile)
                value = jnp.dot(
                    hid[q].reshape(rows, hidden),
                    down_w[half, :, pl.ds(at, tile)],
                    preferred_element_type=F32,
                )
                down_part[q, :, :, :, pl.ds(pl.multiple_of(half * width + at, tile), tile)] = (
                    value.astype(BF16).reshape(n, chips, piece, tile)
                )

        for j in range(1, n):
            down_copies[q].append(
                send(
                    down_part.at[q, lax.rem(me + j, n)],
                    down_recv.at[q, j],
                    down_ss.at[q, j],
                    down_rs.at[q, j],
                    along(j),
                )
            )
    fin_copies = [[] for _ in range(parts)]
    for q in range(parts):
        for copy in down_copies[q]:
            copy.wait_recv()
        value = down_part[q, me].astype(F32)
        for j in range(1, n):
            value = value + down_recv[q, j].astype(F32)
        fin[q] = (upd[q, me] + value).astype(BF16)
        for j in range(1, chips):
            fin_copies[q].append(
                send(fin.at[q, j], fin_recv.at[q, j], fin_ss.at[q, j], fin_rs.at[q, j], back(j))
            )
    for q in range(parts):
        out[q, :, pl.ds(pl.multiple_of(chip * cols, cols), cols)] = fin[q, 0]
        for copy in fin_copies[q]:
            copy.wait_recv()
        for j in range(1, chips):
            start = pl.multiple_of(lax.rem(chip + j, chips) * cols, cols)
            out[q, :, pl.ds(start, cols)] = fin_recv[q, j]

    sent = paired + res_copies + part_copies + stat_copies
    for group in (att_copies, rs_copies, ag_copies, gu_copies, hid_copies, down_copies, fin_copies):
        for copies in group:
            sent = sent + copies
    for copy in sent:
        copy.wait_send()


def local(
    n,
    chips,
    queries,
    fresh_kv,
    kv_pages,
    residual,
    norm_gain,
    out_weight,
    gate_weight,
    up_weight,
    down_weight,
    page_table,
    shared_pages,
    cache_lens,
    prefill_offsets,
):
    own = fresh_kv.shape[1]
    parts = max(1, own // 16)
    piece = own // parts
    width = out_weight.shape[1]
    cols = 2 * width
    feats = out_weight.shape[0]
    hidden = gate_weight.shape[1]
    model = norm_gain.shape[0]
    pool = kv_pages.shape[1] * PAGE
    vmem = pl.BlockSpec(memory_space=pltpu.VMEM)
    anywhere = pl.BlockSpec(memory_space=pl.ANY)

    def dma(*shape):
        return [pltpu.SemaphoreType.DMA(shape)] * 2

    result = pl.pallas_call(
        functools.partial(kernel, n, chips),
        out_shape=jax.ShapeDtypeStruct((parts, piece, model), BF16),
        in_specs=[vmem] * 8 + [anywhere] * 5,
        out_specs=vmem,
        scratch_shapes=[
            pltpu.VMEM((ROWS, pool), F32),
            pltpu.VMEM((ROWS, own), F32),
            pltpu.VMEM((n, ROWS, feats), BF16),
            pltpu.VMEM((n, ROWS, feats), BF16),
            pltpu.VMEM((n, 8, ROWS), F32),
            pltpu.VMEM((n, 8, ROWS), F32),
            pltpu.VMEM((parts, n, chips, piece, cols), BF16),
            pltpu.VMEM((2, feats, width), BF16),
            pltpu.VMEM((2, width, hidden), BF16),
            pltpu.VMEM((2, width, hidden), BF16),
            pltpu.VMEM((2, hidden, width), BF16),
            pltpu.VMEM((parts, n, chips, piece, feats), BF16),
            pltpu.VMEM((parts, n, chips, piece, cols), BF16),
            pltpu.VMEM((parts, n, chips, piece, cols), BF16),
            pltpu.VMEM((parts, n, chips, piece, cols), BF16),
            pltpu.VMEM((parts, n, chips, piece, cols), F32),
            pltpu.VMEM((parts, n, chips, piece, cols), BF16),
            pltpu.VMEM((parts, 2, n, chips, piece, hidden), BF16),
            pltpu.VMEM((parts, chips, 2, n, piece, hidden), BF16),
            pltpu.VMEM((parts, n, chips, piece, HEAD), F32),
            pltpu.VMEM((parts, chips, n, piece, HEAD), F32),
            pltpu.VMEM((parts, n, chips, piece, hidden), BF16),
            pltpu.VMEM((parts, n, chips, piece, cols), BF16),
            pltpu.VMEM((parts, n, chips, piece, cols), BF16),
            pltpu.VMEM((parts, chips, piece, cols), BF16),
            pltpu.VMEM((parts, chips, piece, cols), BF16),
            pltpu.SemaphoreType.DMA((4,)),
            *dma(4),
            pltpu.SemaphoreType.DMA((parts,)),
            *dma(parts, chips),
            *dma(n),
            *dma(n),
            *dma(parts, chips),
            *dma(parts, n),
            *dma(parts, n),
            *dma(parts, chips, 2),
            *dma(parts, chips),
            *dma(parts, chips),
            *dma(parts, n),
            *dma(parts, chips),
        ],
        compiler_params=pltpu.CompilerParams(
            collective_id=0, has_side_effects=True, vmem_limit_bytes=60 * 1024 * 1024
        ),
    )(
        queries[0],
        kv_pages.reshape(pool, kv_pages.shape[3]),
        fresh_kv[0],
        norm_gain[None],
        page_table[0],
        shared_pages,
        cache_lens.reshape(DECODES, 1),
        prefill_offsets.reshape(1, 1),
        residual.reshape(n, parts, piece, model),
        out_weight,
        gate_weight,
        up_weight,
        down_weight,
    )
    return result.reshape(1, own, model)


def solution(mesh):
    placed = (
        P("grp", None, None),
        P("grp", "mlp", None),
        P("grp", "mlp", None, None),
        P("grp", None, None),
        P(),
        P("mlp", "grp"),
        P("grp", "mlp"),
        P("grp", "mlp"),
        P("mlp", "grp"),
        P("grp", None, None),
        P("grp", None),
        P("grp", None),
        P("grp"),
    )
    return jax.shard_map(
        functools.partial(local, mesh.shape["mlp"], mesh.shape["grp"] // 2),
        mesh=mesh,
        in_specs=placed,
        out_specs=P("grp", "mlp", None),
        check_vma=False,
    )
```

```python
import functools

import jax
import jax.numpy as jnp
from jax import lax
from jax.experimental import pallas as pl
from jax.experimental.pallas import tpu as pltpu
from jax.sharding import PartitionSpec as P

HEADS = 32
KV_HEADS = 4
HEAD = 128
PAGE = 128
SHARED_PAGES = 4
PRIVATE_PAGES = 12
DECODES = 16
PREFILL = 112
ROWS = 128
GROUPED = HEADS // KV_HEADS

NEG_FILL = -1e30
EPSILON = 1e-05
MESH = pl.DeviceIdType.MESH
F32 = jnp.float32
BF16 = jnp.bfloat16


def tile_of(width):
    return 256 if width % 256 == 0 else 128


def kernel(
    n,
    chips,
    queries,
    kv_pages,
    fresh_kv,
    gain,
    table,
    shared,
    lens,
    offset,
    residual,
    out_weight,
    gate_weight,
    up_weight,
    down_weight,
    out,
    bias,
    fresh_bias,
    part_send,
    part_recv,
    stat_send,
    stat_recv,
    res,
    out_w,
    gate_w,
    up_w,
    down_w,
    att,
    proj_part,
    proj_recv,
    proj,
    upd,
    normed,
    gu,
    gu_recv,
    ssq,
    ssq_recv,
    hid,
    down_part,
    down_recv,
    fin,
    fin_recv,
    weight_local,
    weight_send,
    weight_recv,
    res_local,
    res_send,
    res_recv,
    part_ss,
    part_rs,
    stat_ss,
    stat_rs,
    att_ss,
    att_rs,
    rs_ss,
    rs_rs,
    ag_ss,
    ag_rs,
    gu_ss,
    gu_rs,
    ssq_ss,
    ssq_rs,
    hid_ss,
    hid_rs,
    down_ss,
    down_rs,
    fin_ss,
    fin_rs,
):
    me = lax.axis_index("mlp")
    grp = lax.axis_index("grp")
    chip = grp // 2
    core = grp % 2
    parts = res.shape[0]
    piece = res.shape[3]
    width = out_w.shape[2]
    cols = 2 * width
    feats = att.shape[-1]
    hidden = hid.shape[-1]
    block_heads = feats // HEAD
    rows = n * chips * piece

    def along(j):
        return {"mlp": lax.rem(me + j, n)}

    def across(j):
        return {"grp": lax.rem(chip + j, chips) * 2 + core}

    def back(j):
        return {"grp": lax.rem(chip + chips - j, chips) * 2 + core}

    partner = {"grp": chip * 2 + (1 - core)}

    def send(src, dst, ss, rs, device):
        copy = pltpu.make_async_remote_copy(
            src_ref=src,
            dst_ref=dst,
            send_sem=ss,
            recv_sem=rs,
            device_id=device,
            device_id_type=MESH,
        )
        copy.start()
        return copy

    barrier = pltpu.get_barrier_semaphore()
    for j in range(1, n):
        pl.semaphore_signal(barrier, inc=1, device_id=along(j), device_id_type=MESH)
    for j in range(1, chips):
        pl.semaphore_signal(barrier, inc=1, device_id=across(j), device_id_type=MESH)
    pl.semaphore_signal(barrier, inc=1, device_id=partner, device_id_type=MESH)

    local_weights = (
        (out_weight, out_w.at[core]),
        (gate_weight, gate_w.at[core]),
        (up_weight, up_w.at[core]),
        (down_weight, down_w.at[core]),
    )
    held = []
    for i, (src, dst) in enumerate(local_weights):
        copy = pltpu.make_async_copy(src, dst, weight_local.at[i])
        copy.start()
        held.append(copy)
    own_res = []
    for q in range(parts):
        copy = pltpu.make_async_copy(
            residual.at[:, q, :, pl.ds(pl.multiple_of(chip * cols, cols), cols)],
            res.at[q, :, 0],
            res_local.at[q],
        )
        copy.start()
        own_res.append(copy)

    pl.semaphore_wait(barrier, n + chips - 1)

    paired = []
    for i, (src, dst) in enumerate(local_weights):
        paired.append(send(src, dst, weight_send.at[i], weight_recv.at[i], partner))
    res_copies = []
    for q in range(parts):
        for j in range(1, chips):
            start = pl.multiple_of(lax.rem(chip + j, chips) * cols, cols)
            res_copies.append(
                send(
                    residual.at[:, q, :, pl.ds(start, cols)],
                    res.at[q, :, j],
                    res_send.at[q, j],
                    res_recv.at[q, j],
                    across(j),
                )
            )

    pool_pages = kv_pages.shape[0] // PAGE
    own_count = fresh_kv.shape[0]
    token = lax.broadcasted_iota(jnp.int32, (1, PAGE), 1)
    slot_ids = lax.broadcasted_iota(jnp.int32, (PRIVATE_PAGES, DECODES), 0)
    shared_ids = lax.broadcasted_iota(jnp.int32, (1, SHARED_PAGES), 1)
    diagonal = lax.broadcasted_iota(jnp.int32, (DECODES, DECODES), 0) == (
        lax.broadcasted_iota(jnp.int32, (DECODES, DECODES), 1)
    )

    def upright(row):
        return jnp.sum(jnp.where(diagonal, row, 0), axis=1, keepdims=True)

    limits = upright(lens[...])
    for p in range(pool_pages):
        page_id = me * pool_pages + p
        own = table[...] == page_id
        own_any = upright(jnp.max(jnp.where(own, 1, 0), axis=0, keepdims=True))
        own_base = upright(
            jnp.sum(
                jnp.where(own, (SHARED_PAGES + slot_ids) * PAGE, 0), axis=0, keepdims=True
            )
        )
        match = shared[...] == page_id
        is_shared = jnp.max(jnp.where(match, 1, 0), axis=1, keepdims=True)
        shared_base = jnp.sum(jnp.where(match, shared_ids * PAGE, 0), axis=1, keepdims=True)
        position = shared_base + token
        seen = (is_shared > 0) & (position < offset[0])
        prefill_bias = jnp.broadcast_to(jnp.where(seen, 0.0, NEG_FILL), (PREFILL, PAGE))
        belongs = jnp.maximum(own_any, is_shared)
        base = jnp.where(is_shared > 0, shared_base, own_base)
        seen = (belongs > 0) & (base + token < limits)
        decode_bias = jnp.where(seen, 0.0, NEG_FILL)
        bias[:, :, :, p * PAGE : (p + 1) * PAGE] = jnp.concatenate(
            [prefill_bias, decode_bias], axis=0
        ).reshape(n, parts, piece, PAGE)
    row_ids = lax.broadcasted_iota(jnp.int32, (ROWS, own_count), 0)
    key_rows = me * own_count + lax.broadcasted_iota(jnp.int32, (ROWS, own_count), 1)
    seen = ((row_ids < PREFILL) & (key_rows < PREFILL) & (key_rows <= row_ids)) | (
        (row_ids >= PREFILL) & (key_rows == row_ids)
    )
    fresh_bias[...] = jnp.where(seen, 0.0, NEG_FILL).reshape(n, parts, piece, own_count)

    scale = HEAD ** (-0.5)
    keys_across = (((1,), (1,)), ((), ()))
    value_at = KV_HEADS * HEAD
    rows_here = n * piece
    stacked = block_heads * rows_here
    lane = lax.broadcasted_iota(jnp.int32, (rows_here, ROWS), 1)

    def part_copy(q, j, block):
        return pltpu.make_async_remote_copy(
            src_ref=part_send.at[q, block],
            dst_ref=part_recv.at[q, j],
            send_sem=part_ss.at[q, j],
            recv_sem=part_rs.at[q, j],
            device_id=along(j),
            device_id_type=MESH,
        )

    def stat_copy(q, j, block):
        return pltpu.make_async_remote_copy(
            src_ref=stat_send.at[q, block],
            dst_ref=stat_recv.at[q, j],
            send_sem=stat_ss.at[q, j],
            recv_sem=stat_rs.at[q, j],
            device_id=along(j),
            device_id_type=MESH,
        )

    for q in range(parts):

        @pl.loop(1, n + 1)
        def _(j, q=q):
            block = lax.rem(me + j, n)
            key_start = pl.multiple_of((block * block_heads // GROUPED) * HEAD, HEAD)
            query = jnp.concatenate(
                [
                    queries[
                        :, q, :, pl.ds(pl.multiple_of((block * block_heads + i) * HEAD, HEAD), HEAD)
                    ].reshape(rows_here, HEAD)
                    for i in range(block_heads)
                ],
                axis=0,
            )
            here = bias[:, q].reshape(1, rows_here, pool_pages * PAGE)
            fresh_here = fresh_bias[:, q].reshape(1, rows_here, own_count)
            scores = lax.dot_general(
                query,
                kv_pages[:, pl.ds(key_start, HEAD)],
                keys_across,
                preferred_element_type=F32,
            )
            scores = scores.reshape(block_heads, rows_here, -1) * scale + here
            fresh_scores = lax.dot_general(
                query,
                fresh_kv[:, pl.ds(key_start, HEAD)],
                keys_across,
                preferred_element_type=F32,
            )
            fresh_scores = fresh_scores.reshape(block_heads, rows_here, -1) * scale + fresh_here
            peak = jnp.maximum(
                jnp.max(scores, axis=2, keepdims=True),
                jnp.max(fresh_scores, axis=2, keepdims=True),
            )
            exps = jnp.exp(scores - peak)
            fresh_exps = jnp.exp(fresh_scores - peak)
            total = jnp.sum(exps, axis=2, keepdims=True) + jnp.sum(
                fresh_exps, axis=2, keepdims=True
            )
            mixed = jnp.dot(
                exps.astype(BF16).reshape(stacked, pool_pages * PAGE),
                kv_pages[:, pl.ds(value_at + key_start, HEAD)],
                preferred_element_type=F32,
            ) + jnp.dot(
                fresh_exps.astype(BF16).reshape(stacked, own_count),
                fresh_kv[:, pl.ds(value_at + key_start, HEAD)],
                preferred_element_type=F32,
            )
            mixed = (mixed.reshape(block_heads, rows_here, HEAD) / total).astype(BF16)
            level = peak + jnp.log(total)
            stats = jnp.zeros((rows_here, ROWS), F32)
            for i in range(block_heads):
                part_send[q, block, :, i * HEAD : (i + 1) * HEAD] = mixed[i]
                stats = jnp.where(lane == i, level[i], stats)
            if rows_here < ROWS:
                stats = jnp.concatenate(
                    [stats, jnp.zeros((ROWS - rows_here, ROWS), F32)], axis=0
                )
            stat_send[q, block] = stats.T[0:8]

            @pl.when(j < n)
            def _():
                part_copy(q, j, block).start()
                stat_copy(q, j, block).start()

    att_copies = [[] for _ in range(parts)]
    for q in range(parts):
        for j in range(1, n):
            stat_copy(q, j, lax.rem(me + j, n)).wait_recv()
            part_copy(q, j, lax.rem(me + j, n)).wait_recv()
        levels = [stat_send[q, me].T] + [stat_recv[q, j].T for j in range(1, n)]
        top = functools.reduce(jnp.maximum, levels)
        shares = [jnp.exp(level - top) for level in levels]
        whole = functools.reduce(jnp.add, shares)
        shares = [share / whole for share in shares]
        for i in range(block_heads):
            span = slice(i * HEAD, (i + 1) * HEAD)
            value = part_send[q, me, :, span].astype(F32) * shares[0][0:rows_here, i : i + 1]
            for j in range(1, n):
                value = value + (
                    part_recv[q, j, :, span].astype(F32) * shares[j][0:rows_here, i : i + 1]
                )
            att[q, :, 0, :, span] = value.astype(BF16).reshape(n, piece, HEAD)
        for j in range(1, chips):
            att_copies[q].append(
                send(att.at[q, :, 0], att.at[q, :, j], att_ss.at[q, j], att_rs.at[q, j], across(j))
            )

    held[0].wait()
    paired[0].wait_recv()
    rs_copies = [[] for _ in range(parts)]
    tile = tile_of(width)
    for q in range(parts):
        for copy in att_copies[q]:
            copy.wait_recv()
        for half in range(2):

            @pl.loop(0, width // tile)
            def _(t, q=q, half=half):
                at = pl.multiple_of(t * tile, tile)
                value = jnp.dot(
                    att[q].reshape(rows, feats),
                    out_w[half, :, pl.ds(at, tile)],
                    preferred_element_type=F32,
                )
                proj_part[q, :, :, :, pl.ds(pl.multiple_of(half * width + at, tile), tile)] = (
                    value.astype(BF16).reshape(n, chips, piece, tile)
                )

        for j in range(1, n):
            rs_copies[q].append(
                send(
                    proj_part.at[q, lax.rem(me + j, n)],
                    proj_recv.at[q, j],
                    rs_ss.at[q, j],
                    rs_rs.at[q, j],
                    along(j),
                )
            )
    ag_copies = [[] for _ in range(parts)]
    for q in range(parts):
        for copy in rs_copies[q]:
            copy.wait_recv()
        value = proj_part[q, me].astype(F32)
        for j in range(1, n):
            value = value + proj_recv[q, j].astype(F32)
        proj[q, me] = value.astype(BF16)
        for j in range(1, n):
            ag_copies[q].append(
                send(proj.at[q, me], proj.at[q, me], ag_ss.at[q, j], ag_rs.at[q, j], along(j))
            )

    for copy in own_res:
        copy.wait()
    for copy in res_copies:
        copy.wait_recv()
    for i in (1, 2):
        held[i].wait()
        paired[i].wait_recv()
    gain_here = gain[:, pl.ds(pl.multiple_of(chip * cols, cols), cols)]
    gu_copies = [[] for _ in range(parts)]
    tile = tile_of(hidden)
    for q in range(parts):
        for j in range(1, n):
            other = lax.rem(me + n - j, n)
            pltpu.make_async_remote_copy(
                src_ref=proj.at[q, other],
                dst_ref=proj.at[q, other],
                send_sem=ag_ss.at[q, j],
                recv_sem=ag_rs.at[q, j],
                device_id=along(j),
                device_id_type=MESH,
            ).wait_recv()

        @pl.loop(0, n)
        def _(p, q=q):
            value = res[q, p].astype(F32) + proj[q, p].astype(F32)
            upd[q, p] = value
            square = jnp.sum(value * value, axis=2, keepdims=True)
            ssq[q, p] = jnp.broadcast_to(square, (chips, piece, HEAD))
            normed[q, p] = (value * gain_here[None]).astype(BF16)

        for j in range(1, chips):
            gu_copies[q].append(
                send(ssq.at[q, :, j], ssq_recv.at[q, j], ssq_ss.at[q, j], ssq_rs.at[q, j], back(j))
            )
        for which, weight in enumerate((gate_w, up_w)):

            @pl.loop(0, hidden // tile)
            def _(t, q=q, which=which, weight=weight):
                at = pl.multiple_of(t * tile, tile)
                value = jnp.dot(
                    normed[q].reshape(rows, cols),
                    weight[:, :, pl.ds(at, tile)].reshape(cols, tile),
                    preferred_element_type=F32,
                )
                gu[q, which, :, :, :, pl.ds(at, tile)] = value.astype(BF16).reshape(
                    n, chips, piece, tile
                )

            for j in range(1, chips):
                gu_copies[q].append(
                    send(
                        gu.at[q, which, :, j],
                        gu_recv.at[q, j, which],
                        gu_ss.at[q, j, which],
                        gu_rs.at[q, j, which],
                        back(j),
                    )
                )

    hid_copies = [[] for _ in range(parts)]
    for q in range(parts):
        for copy in gu_copies[q]:
            copy.wait_recv()

        @pl.loop(0, n)
        def _(p, q=q):
            square = ssq[q, p, 0]
            for j in range(1, chips):
                square = square + ssq_recv[q, j, p]
            factor = lax.rsqrt(square[:, 0:1] / (chips * cols) + EPSILON)
            gate = gu[q, 0, p, 0].astype(F32)
            up = gu[q, 1, p, 0].astype(F32)
            for j in range(1, chips):
                gate = gate + gu_recv[q, j, 0, p].astype(F32)
                up = up + gu_recv[q, j, 1, p].astype(F32)
            gate = gate * factor
            up = up * factor
            hid[q, p, 0] = (gate / (1.0 + jnp.exp(-gate)) * up).astype(BF16)

        for j in range(1, chips):
            hid_copies[q].append(
                send(hid.at[q, :, 0], hid.at[q, :, j], hid_ss.at[q, j], hid_rs.at[q, j], across(j))
            )

    held[3].wait()
    paired[3].wait_recv()
    down_copies = [[] for _ in range(parts)]
    tile = tile_of(width)
    for q in range(parts):
        for copy in hid_copies[q]:
            copy.wait_recv()
        for half in range(2):

            @pl.loop(0, width // tile)
            def _(t, q=q, half=half):
                at = pl.multiple_of(t * tile, tile)
                value = jnp.dot(
                    hid[q].reshape(rows, hidden),
                    down_w[half, :, pl.ds(at, tile)],
                    preferred_element_type=F32,
                )
                down_part[q, :, :, :, pl.ds(pl.multiple_of(half * width + at, tile), tile)] = (
                    value.astype(BF16).reshape(n, chips, piece, tile)
                )

        for j in range(1, n):
            down_copies[q].append(
                send(
                    down_part.at[q, lax.rem(me + j, n)],
                    down_recv.at[q, j],
                    down_ss.at[q, j],
                    down_rs.at[q, j],
                    along(j),
                )
            )
    fin_copies = [[] for _ in range(parts)]
    for q in range(parts):
        for copy in down_copies[q]:
            copy.wait_recv()
        value = down_part[q, me].astype(F32)
        for j in range(1, n):
            value = value + down_recv[q, j].astype(F32)
        fin[q] = (upd[q, me] + value).astype(BF16)
        for j in range(1, chips):
            fin_copies[q].append(
                send(fin.at[q, j], fin_recv.at[q, j], fin_ss.at[q, j], fin_rs.at[q, j], back(j))
            )
    for q in range(parts):
        out[q, :, pl.ds(pl.multiple_of(chip * cols, cols), cols)] = fin[q, 0]
        for copy in fin_copies[q]:
            copy.wait_recv()
        for j in range(1, chips):
            start = pl.multiple_of(lax.rem(chip + j, chips) * cols, cols)
            out[q, :, pl.ds(start, cols)] = fin_recv[q, j]

    sent = paired + res_copies
    for q in range(parts):
        for j in range(1, n):
            sent.append(part_copy(q, j, lax.rem(me + j, n)))
            sent.append(stat_copy(q, j, lax.rem(me + j, n)))
    for group in (att_copies, rs_copies, ag_copies, gu_copies, hid_copies, down_copies, fin_copies):
        for copies in group:
            sent = sent + copies
    for copy in sent:
        copy.wait_send()


def local(
    n,
    chips,
    queries,
    fresh_kv,
    kv_pages,
    residual,
    norm_gain,
    out_weight,
    gate_weight,
    up_weight,
    down_weight,
    page_table,
    shared_pages,
    cache_lens,
    prefill_offsets,
):
    own = fresh_kv.shape[1]
    parts = max(1, own // 16)
    piece = own // parts
    width = out_weight.shape[1]
    cols = 2 * width
    feats = out_weight.shape[0]
    hidden = gate_weight.shape[1]
    model = norm_gain.shape[0]
    pool = kv_pages.shape[1] * PAGE
    vmem = pl.BlockSpec(memory_space=pltpu.VMEM)
    anywhere = pl.BlockSpec(memory_space=pl.ANY)

    def dma(*shape):
        return [pltpu.SemaphoreType.DMA(shape)] * 2

    result = pl.pallas_call(
        functools.partial(kernel, n, chips),
        out_shape=jax.ShapeDtypeStruct((parts, piece, model), BF16),
        in_specs=[vmem] * 7 + [pl.BlockSpec(memory_space=pltpu.SMEM)] + [anywhere] * 5,
        out_specs=vmem,
        scratch_shapes=[
            pltpu.VMEM((n, parts, piece, pool), F32),
            pltpu.VMEM((n, parts, piece, own), F32),
            pltpu.VMEM((parts, n, n * piece, feats), BF16),
            pltpu.VMEM((parts, n, n * piece, feats), BF16),
            pltpu.VMEM((parts, n, 8, ROWS), F32),
            pltpu.VMEM((parts, n, 8, ROWS), F32),
            pltpu.VMEM((parts, n, chips, piece, cols), BF16),
            pltpu.VMEM((2, feats, width), BF16),
            pltpu.VMEM((2, width, hidden), BF16),
            pltpu.VMEM((2, width, hidden), BF16),
            pltpu.VMEM((2, hidden, width), BF16),
            pltpu.VMEM((parts, n, chips, piece, feats), BF16),
            pltpu.VMEM((parts, n, chips, piece, cols), BF16),
            pltpu.VMEM((parts, n, chips, piece, cols), BF16),
            pltpu.VMEM((parts, n, chips, piece, cols), BF16),
            pltpu.VMEM((parts, n, chips, piece, cols), F32),
            pltpu.VMEM((parts, n, chips, piece, cols), BF16),
            pltpu.VMEM((parts, 2, n, chips, piece, hidden), BF16),
            pltpu.VMEM((parts, chips, 2, n, piece, hidden), BF16),
            pltpu.VMEM((parts, n, chips, piece, HEAD), F32),
            pltpu.VMEM((parts, chips, n, piece, HEAD), F32),
            pltpu.VMEM((parts, n, chips, piece, hidden), BF16),
            pltpu.VMEM((parts, n, chips, piece, cols), BF16),
            pltpu.VMEM((parts, n, chips, piece, cols), BF16),
            pltpu.VMEM((parts, chips, piece, cols), BF16),
            pltpu.VMEM((parts, chips, piece, cols), BF16),
            pltpu.SemaphoreType.DMA((4,)),
            *dma(4),
            pltpu.SemaphoreType.DMA((parts,)),
            *dma(parts, chips),
            *dma(parts, n),
            *dma(parts, n),
            *dma(parts, chips),
            *dma(parts, n),
            *dma(parts, n),
            *dma(parts, chips, 2),
            *dma(parts, chips),
            *dma(parts, chips),
            *dma(parts, n),
            *dma(parts, chips),
        ],
        compiler_params=pltpu.CompilerParams(
            collective_id=0, has_side_effects=True, vmem_limit_bytes=60 * 1024 * 1024
        ),
    )(
        queries.reshape(n, parts, piece, queries.shape[2]),
        kv_pages.reshape(pool, kv_pages.shape[3]),
        fresh_kv[0],
        norm_gain[None],
        page_table[0].T,
        shared_pages,
        cache_lens,
        prefill_offsets,
        residual.reshape(n, parts, piece, model),
        out_weight,
        gate_weight,
        up_weight,
        down_weight,
    )
    return result.reshape(1, own, model)


def solution(mesh):
    placed = (
        P("grp", None, None),
        P("grp", "mlp", None),
        P("grp", "mlp", None, None),
        P("grp", None, None),
        P(),
        P("mlp", "grp"),
        P("grp", "mlp"),
        P("grp", "mlp"),
        P("mlp", "grp"),
        P("grp", None, None),
        P("grp", None),
        P("grp", None),
        P("grp"),
    )
    return jax.shard_map(
        functools.partial(local, mesh.shape["mlp"], mesh.shape["grp"] // 2),
        mesh=mesh,
        in_specs=placed,
        out_specs=P("grp", "mlp", None),
        check_vma=False,
    )
```

```python
import functools

import jax
import jax.numpy as jnp
from jax import lax
from jax.experimental import pallas as pl
from jax.experimental.pallas import tpu as pltpu
from jax.sharding import PartitionSpec as P

HEADS = 32
KV_HEADS = 4
HEAD = 128
PAGE = 128
SHARED_PAGES = 4
PRIVATE_PAGES = 12
DECODES = 16
PREFILL = 112
ROWS = 128
GROUPED = HEADS // KV_HEADS

NEG_FILL = -1e30
EPSILON = 1e-05
MESH = pl.DeviceIdType.MESH
F32 = jnp.float32
BF16 = jnp.bfloat16


def tile_of(width):
    return 256 if width % 256 == 0 else 128


def kernel(
    n,
    chips,
    queries,
    kv_pages,
    fresh_kv,
    gain,
    table,
    shared,
    lens,
    offset,
    residual,
    out_weight,
    gate_weight,
    up_weight,
    down_weight,
    out,
    bias,
    fresh_bias,
    part_send,
    part_recv,
    stat_send,
    stat_recv,
    res,
    out_w,
    gate_w,
    up_w,
    down_w,
    att,
    proj_part,
    proj_recv,
    proj,
    upd,
    normed,
    gu,
    gu_recv,
    ssq,
    ssq_recv,
    hid,
    down_part,
    down_recv,
    fin,
    fin_recv,
    weight_local,
    weight_send,
    weight_recv,
    res_local,
    res_send,
    res_recv,
    part_ss,
    part_rs,
    stat_ss,
    stat_rs,
    att_ss,
    att_rs,
    rs_ss,
    rs_rs,
    ag_ss,
    ag_rs,
    gu_ss,
    gu_rs,
    ssq_ss,
    ssq_rs,
    hid_ss,
    hid_rs,
    down_ss,
    down_rs,
    fin_ss,
    fin_rs,
):
    me = lax.axis_index("mlp")
    grp = lax.axis_index("grp")
    chip = grp // 2
    core = grp % 2
    parts = res.shape[0]
    piece = res.shape[3]
    width = out_w.shape[2]
    cols = 2 * width
    feats = att.shape[-1]
    hidden = hid.shape[-1]
    block_heads = feats // HEAD
    rows = n * chips * piece

    def along(j):
        return {"mlp": lax.rem(me + j, n)}

    def across(j):
        return {"grp": lax.rem(chip + j, chips) * 2 + core}

    def back(j):
        return {"grp": lax.rem(chip + chips - j, chips) * 2 + core}

    partner = {"grp": chip * 2 + (1 - core)}

    def send(src, dst, ss, rs, device):
        copy = pltpu.make_async_remote_copy(
            src_ref=src,
            dst_ref=dst,
            send_sem=ss,
            recv_sem=rs,
            device_id=device,
            device_id_type=MESH,
        )
        copy.start()
        return copy

    barrier = pltpu.get_barrier_semaphore()
    for j in range(1, n):
        pl.semaphore_signal(barrier, inc=1, device_id=along(j), device_id_type=MESH)
    for j in range(1, chips):
        pl.semaphore_signal(barrier, inc=1, device_id=across(j), device_id_type=MESH)
    pl.semaphore_signal(barrier, inc=1, device_id=partner, device_id_type=MESH)

    local_weights = (
        (out_weight, out_w.at[core]),
        (gate_weight, gate_w.at[core]),
        (up_weight, up_w.at[core]),
        (down_weight, down_w.at[core]),
    )
    held = []
    for i, (src, dst) in enumerate(local_weights):
        copy = pltpu.make_async_copy(src, dst, weight_local.at[i])
        copy.start()
        held.append(copy)
    own_res = []
    for q in range(parts):
        copy = pltpu.make_async_copy(
            residual.at[:, q, :, pl.ds(pl.multiple_of(chip * cols, cols), cols)],
            res.at[q, :, 0],
            res_local.at[q],
        )
        copy.start()
        own_res.append(copy)

    pl.semaphore_wait(barrier, n + chips - 1)

    paired = []
    for i, (src, dst) in enumerate(local_weights):
        paired.append(send(src, dst, weight_send.at[i], weight_recv.at[i], partner))
    res_copies = []
    for q in range(parts):
        for j in range(1, chips):
            start = pl.multiple_of(lax.rem(chip + j, chips) * cols, cols)
            res_copies.append(
                send(
                    residual.at[:, q, :, pl.ds(start, cols)],
                    res.at[q, :, j],
                    res_send.at[q, j],
                    res_recv.at[q, j],
                    across(j),
                )
            )

    pool_pages = kv_pages.shape[0] // PAGE
    own_count = fresh_kv.shape[0]
    token = lax.broadcasted_iota(jnp.int32, (1, PAGE), 1)
    slot_ids = lax.broadcasted_iota(jnp.int32, (PRIVATE_PAGES, DECODES), 0)
    shared_ids = lax.broadcasted_iota(jnp.int32, (1, SHARED_PAGES), 1)
    diagonal = lax.broadcasted_iota(jnp.int32, (DECODES, DECODES), 0) == (
        lax.broadcasted_iota(jnp.int32, (DECODES, DECODES), 1)
    )

    def upright(row):
        return jnp.sum(jnp.where(diagonal, row, 0), axis=1, keepdims=True)

    limits = upright(lens[...])
    for p in range(pool_pages):
        page_id = me * pool_pages + p
        own = table[...] == page_id
        own_any = upright(jnp.max(jnp.where(own, 1, 0), axis=0, keepdims=True))
        own_base = upright(
            jnp.sum(
                jnp.where(own, (SHARED_PAGES + slot_ids) * PAGE, 0), axis=0, keepdims=True
            )
        )
        match = shared[...] == page_id
        is_shared = jnp.max(jnp.where(match, 1, 0), axis=1, keepdims=True)
        shared_base = jnp.sum(jnp.where(match, shared_ids * PAGE, 0), axis=1, keepdims=True)
        position = shared_base + token
        seen = (is_shared > 0) & (position < offset[0])
        prefill_bias = jnp.broadcast_to(jnp.where(seen, 0.0, NEG_FILL), (PREFILL, PAGE))
        belongs = jnp.maximum(own_any, is_shared)
        base = jnp.where(is_shared > 0, shared_base, own_base)
        seen = (belongs > 0) & (base + token < limits)
        decode_bias = jnp.where(seen, 0.0, NEG_FILL)
        bias[:, :, :, p * PAGE : (p + 1) * PAGE] = jnp.concatenate(
            [prefill_bias, decode_bias], axis=0
        ).reshape(n, parts, piece, PAGE)
    row_ids = lax.broadcasted_iota(jnp.int32, (ROWS, own_count), 0)
    key_rows = me * own_count + lax.broadcasted_iota(jnp.int32, (ROWS, own_count), 1)
    seen = ((row_ids < PREFILL) & (key_rows < PREFILL) & (key_rows <= row_ids)) | (
        (row_ids >= PREFILL) & (key_rows == row_ids)
    )
    fresh_bias[...] = jnp.where(seen, 0.0, NEG_FILL).reshape(n, parts, piece, own_count)

    scale = HEAD ** (-0.5)
    keys_across = (((1,), (1,)), ((), ()))
    value_at = KV_HEADS * HEAD
    rows_here = n * piece
    stacked = block_heads * rows_here
    lane = lax.broadcasted_iota(jnp.int32, (rows_here, ROWS), 1)

    def part_copy(q, j, block):
        return pltpu.make_async_remote_copy(
            src_ref=part_send.at[q, block],
            dst_ref=part_recv.at[q, j],
            send_sem=part_ss.at[q, j],
            recv_sem=part_rs.at[q, j],
            device_id=along(j),
            device_id_type=MESH,
        )

    def stat_copy(q, j, block):
        return pltpu.make_async_remote_copy(
            src_ref=stat_send.at[q, block],
            dst_ref=stat_recv.at[q, j],
            send_sem=stat_ss.at[q, j],
            recv_sem=stat_rs.at[q, j],
            device_id=along(j),
            device_id_type=MESH,
        )

    for q in range(parts):

        @pl.loop(1, n + 1)
        def _(j, q=q):
            block = lax.rem(me + j, n)
            key_start = pl.multiple_of((block * block_heads // GROUPED) * HEAD, HEAD)
            query = jnp.concatenate(
                [
                    queries[
                        :, q, :, pl.ds(pl.multiple_of((block * block_heads + i) * HEAD, HEAD), HEAD)
                    ].reshape(rows_here, HEAD)
                    for i in range(block_heads)
                ],
                axis=0,
            )
            here = bias[:, q].reshape(1, rows_here, pool_pages * PAGE)
            fresh_here = fresh_bias[:, q].reshape(1, rows_here, own_count)
            scores = lax.dot_general(
                query,
                kv_pages[:, pl.ds(key_start, HEAD)],
                keys_across,
                preferred_element_type=F32,
            )
            scores = scores.reshape(block_heads, rows_here, -1) * scale + here
            fresh_scores = lax.dot_general(
                query,
                fresh_kv[:, pl.ds(key_start, HEAD)],
                keys_across,
                preferred_element_type=F32,
            )
            fresh_scores = fresh_scores.reshape(block_heads, rows_here, -1) * scale + fresh_here
            peak = jnp.maximum(
                jnp.max(scores, axis=2, keepdims=True),
                jnp.max(fresh_scores, axis=2, keepdims=True),
            )
            exps = jnp.exp(scores - peak)
            fresh_exps = jnp.exp(fresh_scores - peak)
            total = jnp.sum(exps, axis=2, keepdims=True) + jnp.sum(
                fresh_exps, axis=2, keepdims=True
            )
            mixed = jnp.dot(
                exps.astype(BF16).reshape(stacked, pool_pages * PAGE),
                kv_pages[:, pl.ds(value_at + key_start, HEAD)],
                preferred_element_type=F32,
            ) + jnp.dot(
                fresh_exps.astype(BF16).reshape(stacked, own_count),
                fresh_kv[:, pl.ds(value_at + key_start, HEAD)],
                preferred_element_type=F32,
            )
            mixed = (mixed.reshape(block_heads, rows_here, HEAD) / total).astype(BF16)
            level = peak + jnp.log(total)
            stats = jnp.zeros((rows_here, ROWS), F32)
            for i in range(block_heads):
                part_send[q, block, :, i * HEAD : (i + 1) * HEAD] = mixed[i]
                stats = jnp.where(lane == i, level[i], stats)
            if rows_here < ROWS:
                stats = jnp.concatenate(
                    [stats, jnp.zeros((ROWS - rows_here, ROWS), F32)], axis=0
                )
            stat_send[q, block] = stats.T[0:8]

            @pl.when(j < n)
            def _():
                part_copy(q, j, block).start()
                stat_copy(q, j, block).start()

    att_copies = [[] for _ in range(parts)]
    for q in range(parts):
        for j in range(1, n):
            stat_copy(q, j, lax.rem(me + j, n)).wait_recv()
            part_copy(q, j, lax.rem(me + j, n)).wait_recv()
        levels = [stat_send[q, me].T] + [stat_recv[q, j].T for j in range(1, n)]
        top = functools.reduce(jnp.maximum, levels)
        shares = [jnp.exp(level - top) for level in levels]
        whole = functools.reduce(jnp.add, shares)
        shares = [share / whole for share in shares]
        for i in range(block_heads):
            span = slice(i * HEAD, (i + 1) * HEAD)
            value = part_send[q, me, :, span].astype(F32) * shares[0][0:rows_here, i : i + 1]
            for j in range(1, n):
                value = value + (
                    part_recv[q, j, :, span].astype(F32) * shares[j][0:rows_here, i : i + 1]
                )
            att[q, :, 0, :, span] = value.astype(BF16).reshape(n, piece, HEAD)
        for j in range(1, chips):
            att_copies[q].append(
                send(att.at[q, :, 0], att.at[q, :, j], att_ss.at[q, j], att_rs.at[q, j], across(j))
            )

    held[0].wait()
    paired[0].wait_recv()
    rs_copies = [[] for _ in range(parts)]
    tile = tile_of(width)
    for q in range(parts):
        for copy in att_copies[q]:
            copy.wait_recv()
        for half in range(2):

            @pl.loop(0, width // tile)
            def _(t, q=q, half=half):
                at = pl.multiple_of(t * tile, tile)
                value = jnp.dot(
                    att[q].reshape(rows, feats),
                    out_w[half, :, pl.ds(at, tile)],
                    preferred_element_type=F32,
                )
                proj_part[q, :, :, :, pl.ds(pl.multiple_of(half * width + at, tile), tile)] = (
                    value.astype(BF16).reshape(n, chips, piece, tile)
                )

        for j in range(1, n):
            rs_copies[q].append(
                send(
                    proj_part.at[q, lax.rem(me + j, n)],
                    proj_recv.at[q, j],
                    rs_ss.at[q, j],
                    rs_rs.at[q, j],
                    along(j),
                )
            )
    ag_copies = [[] for _ in range(parts)]
    for q in range(parts):
        for copy in rs_copies[q]:
            copy.wait_recv()
        value = proj_part[q, me].astype(F32)
        for j in range(1, n):
            value = value + proj_recv[q, j].astype(F32)
        proj[q, me] = value.astype(BF16)
        for j in range(1, n):
            ag_copies[q].append(
                send(proj.at[q, me], proj.at[q, me], ag_ss.at[q, j], ag_rs.at[q, j], along(j))
            )

    for copy in own_res:
        copy.wait()
    for copy in res_copies:
        copy.wait_recv()
    for i in (1, 2):
        held[i].wait()
        paired[i].wait_recv()
    gain_here = gain[:, pl.ds(pl.multiple_of(chip * cols, cols), cols)]
    gu_copies = [[] for _ in range(parts)]
    tile = tile_of(hidden)
    for q in range(parts):
        for j in range(1, n):
            other = lax.rem(me + n - j, n)
            pltpu.make_async_remote_copy(
                src_ref=proj.at[q, other],
                dst_ref=proj.at[q, other],
                send_sem=ag_ss.at[q, j],
                recv_sem=ag_rs.at[q, j],
                device_id=along(j),
                device_id_type=MESH,
            ).wait_recv()

        @pl.loop(0, n)
        def _(p, q=q):
            value = res[q, p].astype(F32) + proj[q, p].astype(F32)
            upd[q, p] = value
            square = jnp.sum(value * value, axis=2, keepdims=True)
            ssq[q, p] = jnp.broadcast_to(square, (chips, piece, HEAD))
            normed[q, p] = (value * gain_here[None]).astype(BF16)

        for j in range(1, chips):
            gu_copies[q].append(
                send(ssq.at[q, :, j], ssq_recv.at[q, j], ssq_ss.at[q, j], ssq_rs.at[q, j], back(j))
            )
        for which, weight in enumerate((gate_w, up_w)):

            @pl.loop(0, hidden // tile)
            def _(t, q=q, which=which, weight=weight):
                at = pl.multiple_of(t * tile, tile)
                value = jnp.dot(
                    normed[q].reshape(rows, cols),
                    weight[:, :, pl.ds(at, tile)].reshape(cols, tile),
                    preferred_element_type=F32,
                )
                gu[q, which, :, :, :, pl.ds(at, tile)] = value.astype(BF16).reshape(
                    n, chips, piece, tile
                )

            for j in range(1, chips):
                gu_copies[q].append(
                    send(
                        gu.at[q, which, :, j],
                        gu_recv.at[q, j, which],
                        gu_ss.at[q, j, which],
                        gu_rs.at[q, j, which],
                        back(j),
                    )
                )

    hid_copies = [[] for _ in range(parts)]
    for q in range(parts):
        for copy in gu_copies[q]:
            copy.wait_recv()

        @pl.loop(0, n)
        def _(p, q=q):
            square = ssq[q, p, 0]
            for j in range(1, chips):
                square = square + ssq_recv[q, j, p]
            factor = lax.rsqrt(square[:, 0:1] / (chips * cols) + EPSILON)
            gate = gu[q, 0, p, 0].astype(F32)
            up = gu[q, 1, p, 0].astype(F32)
            for j in range(1, chips):
                gate = gate + gu_recv[q, j, 0, p].astype(F32)
                up = up + gu_recv[q, j, 1, p].astype(F32)
            gate = gate * factor
            up = up * factor
            hid[q, p, 0] = (gate / (1.0 + jnp.exp(-gate)) * up).astype(BF16)

        for j in range(1, chips):
            hid_copies[q].append(
                send(hid.at[q, :, 0], hid.at[q, :, j], hid_ss.at[q, j], hid_rs.at[q, j], across(j))
            )

    held[3].wait()
    paired[3].wait_recv()
    down_copies = [[] for _ in range(parts)]
    tile = tile_of(width)
    for q in range(parts):
        for copy in hid_copies[q]:
            copy.wait_recv()
        for half in range(2):

            @pl.loop(0, width // tile)
            def _(t, q=q, half=half):
                at = pl.multiple_of(t * tile, tile)
                value = jnp.dot(
                    hid[q].reshape(rows, hidden),
                    down_w[half, :, pl.ds(at, tile)],
                    preferred_element_type=F32,
                )
                down_part[q, :, :, :, pl.ds(pl.multiple_of(half * width + at, tile), tile)] = (
                    value.astype(BF16).reshape(n, chips, piece, tile)
                )

        for j in range(1, n):
            down_copies[q].append(
                send(
                    down_part.at[q, lax.rem(me + j, n)],
                    down_recv.at[q, j],
                    down_ss.at[q, j],
                    down_rs.at[q, j],
                    along(j),
                )
            )
    fin_copies = [[] for _ in range(parts)]
    for q in range(parts):
        for copy in down_copies[q]:
            copy.wait_recv()
        value = down_part[q, me].astype(F32)
        for j in range(1, n):
            value = value + down_recv[q, j].astype(F32)
        fin[q] = (upd[q, me] + value).astype(BF16)
        for j in range(1, chips):
            fin_copies[q].append(
                send(fin.at[q, j], fin_recv.at[q, j], fin_ss.at[q, j], fin_rs.at[q, j], back(j))
            )
    for q in range(parts):
        out[q, :, pl.ds(pl.multiple_of(chip * cols, cols), cols)] = fin[q, 0]
        for copy in fin_copies[q]:
            copy.wait_recv()
        for j in range(1, chips):
            start = pl.multiple_of(lax.rem(chip + j, chips) * cols, cols)
            out[q, :, pl.ds(start, cols)] = fin_recv[q, j]

    sent = paired + res_copies
    for q in range(parts):
        for j in range(1, n):
            sent.append(part_copy(q, j, lax.rem(me + j, n)))
            sent.append(stat_copy(q, j, lax.rem(me + j, n)))
    for group in (att_copies, rs_copies, ag_copies, gu_copies, hid_copies, down_copies, fin_copies):
        for copies in group:
            sent = sent + copies
    for copy in sent:
        copy.wait_send()


def local(
    n,
    chips,
    queries,
    fresh_kv,
    kv_pages,
    residual,
    norm_gain,
    out_weight,
    gate_weight,
    up_weight,
    down_weight,
    page_table,
    shared_pages,
    cache_lens,
    prefill_offsets,
):
    own = fresh_kv.shape[1]
    parts = max(1, own // 8)
    piece = own // parts
    width = out_weight.shape[1]
    cols = 2 * width
    feats = out_weight.shape[0]
    hidden = gate_weight.shape[1]
    model = norm_gain.shape[0]
    pool = kv_pages.shape[1] * PAGE
    vmem = pl.BlockSpec(memory_space=pltpu.VMEM)
    anywhere = pl.BlockSpec(memory_space=pl.ANY)

    def dma(*shape):
        return [pltpu.SemaphoreType.DMA(shape)] * 2

    result = pl.pallas_call(
        functools.partial(kernel, n, chips),
        out_shape=jax.ShapeDtypeStruct((parts, piece, model), BF16),
        in_specs=[vmem] * 7 + [pl.BlockSpec(memory_space=pltpu.SMEM)] + [anywhere] * 5,
        out_specs=vmem,
        scratch_shapes=[
            pltpu.VMEM((n, parts, piece, pool), F32),
            pltpu.VMEM((n, parts, piece, own), F32),
            pltpu.VMEM((parts, n, n * piece, feats), BF16),
            pltpu.VMEM((parts, n, n * piece, feats), BF16),
            pltpu.VMEM((parts, n, 8, ROWS), F32),
            pltpu.VMEM((parts, n, 8, ROWS), F32),
            pltpu.VMEM((parts, n, chips, piece, cols), BF16),
            pltpu.VMEM((2, feats, width), BF16),
            pltpu.VMEM((2, width, hidden), BF16),
            pltpu.VMEM((2, width, hidden), BF16),
            pltpu.VMEM((2, hidden, width), BF16),
            pltpu.VMEM((parts, n, chips, piece, feats), BF16),
            pltpu.VMEM((parts, n, chips, piece, cols), BF16),
            pltpu.VMEM((parts, n, chips, piece, cols), BF16),
            pltpu.VMEM((parts, n, chips, piece, cols), BF16),
            pltpu.VMEM((parts, n, chips, piece, cols), F32),
            pltpu.VMEM((parts, n, chips, piece, cols), BF16),
            pltpu.VMEM((parts, 2, n, chips, piece, hidden), BF16),
            pltpu.VMEM((parts, chips, 2, n, piece, hidden), BF16),
            pltpu.VMEM((parts, n, chips, piece, HEAD), F32),
            pltpu.VMEM((parts, chips, n, piece, HEAD), F32),
            pltpu.VMEM((parts, n, chips, piece, hidden), BF16),
            pltpu.VMEM((parts, n, chips, piece, cols), BF16),
            pltpu.VMEM((parts, n, chips, piece, cols), BF16),
            pltpu.VMEM((parts, chips, piece, cols), BF16),
            pltpu.VMEM((parts, chips, piece, cols), BF16),
            pltpu.SemaphoreType.DMA((4,)),
            *dma(4),
            pltpu.SemaphoreType.DMA((parts,)),
            *dma(parts, chips),
            *dma(parts, n),
            *dma(parts, n),
            *dma(parts, chips),
            *dma(parts, n),
            *dma(parts, n),
            *dma(parts, chips, 2),
            *dma(parts, chips),
            *dma(parts, chips),
            *dma(parts, n),
            *dma(parts, chips),
        ],
        compiler_params=pltpu.CompilerParams(
            collective_id=0, has_side_effects=True, vmem_limit_bytes=60 * 1024 * 1024
        ),
    )(
        queries.reshape(n, parts, piece, queries.shape[2]),
        kv_pages.reshape(pool, kv_pages.shape[3]),
        fresh_kv[0],
        norm_gain[None],
        page_table[0].T,
        shared_pages,
        cache_lens,
        prefill_offsets,
        residual.reshape(n, parts, piece, model),
        out_weight,
        gate_weight,
        up_weight,
        down_weight,
    )
    return result.reshape(1, own, model)


def solution(mesh):
    placed = (
        P("grp", None, None),
        P("grp", "mlp", None),
        P("grp", "mlp", None, None),
        P("grp", None, None),
        P(),
        P("mlp", "grp"),
        P("grp", "mlp"),
        P("grp", "mlp"),
        P("mlp", "grp"),
        P("grp", None, None),
        P("grp", None),
        P("grp", None),
        P("grp"),
    )
    return jax.shard_map(
        functools.partial(local, mesh.shape["mlp"], mesh.shape["grp"] // 2),
        mesh=mesh,
        in_specs=placed,
        out_specs=P("grp", "mlp", None),
        check_vma=False,
    )
```
